32 devices in a mesh: groups: 2 (over x), rep: 16 (over z, y, core).
Axes of the slice: x: 2, y: 2, z: 4, core: 2. Of those that a mesh axis runs over, the one named last changes fastest.
Arguments:
- normed_input_rows: bfloat16 [256, 8192], P(('groups', 'rep')), parts along dimension 0, may hold values from -6 to 6
- counts: int32 [32, 8], P('groups'), parts along dimension 0, may hold values from 0 to 8, as said below
- gate_weight_matrix: bfloat16 [8192, 28672], P(None, 'rep'), may hold values from -0.0625 to 0.0625
- up_weight_matrix: bfloat16 [8192, 28672], P(None, 'rep'), may hold values from -0.0625 to 0.0625
- adapter_down_weight: bfloat16 [16, 8192, 128], P('groups', 'rep'), parts along dimension 0, may hold values from -0.0625 to 0.0625
- adapter_gate_weight: bfloat16 [16, 64, 28672], P('groups', None, 'rep'), parts along dimension 0, may hold values from -0.75 to 0.75
- adapter_up_weight: bfloat16 [16, 64, 28672], P('groups', None, 'rep'), parts along dimension 0, may hold values from -0.75 to 0.75
Outputs:
- hidden: bfloat16 [256, 28672], P('groups', 'rep'), parts along dimension 0
The draws below stay inside these ranges and needn't reach their ends.
There are 2 independent parts, one for each index of `groups`. The reference program is written for one: setup_inputs(seed, part) draws one part's arguments, and reference() takes and returns one part's arrays. A program takes and returns all parts, laid end to end along the dimension named above; an argument that names none is the same for every part. Nothing has to cross between parts.
Inputs may be any that keep to these rules, and one draw needn't show every extreme that they name: Each row of counts sums to 8; a replica's rows stand in order of version.
All inputs are finite; a program needn't handle non-finite values.
Results may differ from the reference program's by a relative error of at most 0.0056.
Values may be sent and summed in bfloat16 or wider, within the bound.
No kernel may reach another device: no remote copies, remote signals or barrier semaphores. Data moves between devices by JAX's collectives and lax.ppermute only.
A program may use at most 192 MiB of HBM per device.

```python
import jax
import jax.numpy as jnp

MODEL_WIDTH = 8192
HIDDEN_UNITS = 28672
ADAPTER_RANK = 64
POLICY_VERSIONS = 8
ROWS_DEV = 8
ROWS = 128
N_REP = 16


def draw_counts(key, part):
    key = jax.random.fold_in(key, 1)
    key_one, key_two, key_three, key_four = jax.random.split(key, 4)
    first = jax.random.randint(key_one, (N_REP, ROWS_DEV), 0, POLICY_VERSIONS)
    second = jax.random.randint(key_two, (N_REP, ROWS_DEV), 0, POLICY_VERSIONS)
    order = jax.random.permutation(key_three, POLICY_VERSIONS)
    version = order[jnp.minimum(first, second)]
    chosen = jax.random.randint(key_four, (), 0, N_REP)
    replica = jnp.arange(N_REP, dtype=jnp.int32)[:, None]
    version = jnp.where(replica == chosen, order[0], version)
    table = (version[:, :, None] == jnp.arange(POLICY_VERSIONS, dtype=jnp.int32)[None, None, :]).astype(jnp.int32)
    return jnp.sum(table, axis=1).astype(jnp.int32)


def block_levels(key, dims, cuts, least, largest):
    level = 1.0
    for dim, parts in cuts:
        steps = jax.random.uniform(jax.random.fold_in(jax.random.fold_in(key, 6), dim), (parts,), jnp.float32, least / len(cuts), largest / len(cuts))
        level = level * jnp.repeat(jnp.exp(steps), dims[dim] // parts).reshape((-1,) + (1,) * (len(dims) - 1 - dim))
    return level


def bell_draw(stream_key, dims, spread, reach, shards=(), kind=jnp.bfloat16):
    array = jax.random.normal(stream_key, dims, jnp.float32) * spread
    if len(shards) > 0:
        array = block_levels(stream_key, dims, shards, -0.22, 0.18) * array
    return jnp.clip(array, min=-reach, max=reach).astype(kind)


def setup_inputs(seed: int = 0, part: int = 0) -> dict:
    streams_of = jax.random.split(jax.random.key(seed), 8)
    part_splits = jax.random.split(jax.random.fold_in(streams_of[7], part), 8)
    normed_input_rows = bell_draw(part_splits[0], (ROWS, MODEL_WIDTH), 1.0, 6.0, ((0, 16),))
    counts = draw_counts(jax.random.fold_in(jax.random.fold_in(streams_of[7], part), 71), part)
    gate_weight_matrix = bell_draw(streams_of[2], (MODEL_WIDTH, HIDDEN_UNITS), MODEL_WIDTH ** -0.5, 0.0625, ((1, 16),))
    up_weight_matrix = bell_draw(streams_of[3], (MODEL_WIDTH, HIDDEN_UNITS), MODEL_WIDTH ** -0.5, 0.0625, ((1, 16),))
    adapter_down_weight = bell_draw(part_splits[4], (POLICY_VERSIONS, MODEL_WIDTH, 2 * ADAPTER_RANK), MODEL_WIDTH ** -0.5, 0.0625, ((1, 16),))
    adapter_gate_weight = bell_draw(part_splits[5], (POLICY_VERSIONS, ADAPTER_RANK, HIDDEN_UNITS), ADAPTER_RANK ** -0.5, 0.75, ((2, 16),))
    adapter_up_weight = bell_draw(part_splits[6], (POLICY_VERSIONS, ADAPTER_RANK, HIDDEN_UNITS), ADAPTER_RANK ** -0.5, 0.75, ((2, 16),))
    return dict(normed_input_rows=normed_input_rows, counts=counts, gate_weight_matrix=gate_weight_matrix, up_weight_matrix=up_weight_matrix, adapter_down_weight=adapter_down_weight, adapter_gate_weight=adapter_gate_weight, adapter_up_weight=adapter_up_weight)


adapter_scale = 2.0


def row_versions(counts):
    running = jnp.cumsum(counts, axis=1)
    place = jnp.arange(ROWS_DEV, dtype=jnp.int32)
    version = jnp.sum((running[:, None, :] <= place[None, :, None]).astype(jnp.int32), axis=2)
    return version.reshape(-1)


def reference(normed_input_rows, counts, gate_weight_matrix, up_weight_matrix, adapter_down_weight, adapter_gate_weight, adapter_up_weight):
    version = row_versions(counts)
    onehot = (version[:, None] == jnp.arange(POLICY_VERSIONS, dtype=jnp.int32)[None, :]).astype(jnp.float32)
    every_version_output = jnp.einsum('tj,bjo->tbo', normed_input_rows.astype(jnp.float32), adapter_down_weight.astype(jnp.float32))
    shrink = jnp.sum(every_version_output * onehot[:, :, None], axis=1).astype(jnp.bfloat16)
    expanded_gate = (onehot[:, :, None] * shrink[None, :, :ADAPTER_RANK].reshape(-1, 1, ADAPTER_RANK).astype(jnp.float32)).reshape(-1, POLICY_VERSIONS * ADAPTER_RANK).astype(jnp.bfloat16)
    expanded_up = (onehot[:, :, None] * shrink[:, ADAPTER_RANK:].reshape(-1, 1, ADAPTER_RANK).astype(jnp.float32)).reshape(-1, POLICY_VERSIONS * ADAPTER_RANK).astype(jnp.bfloat16)
    gate_output = jnp.dot(normed_input_rows, gate_weight_matrix, preferred_element_type=jnp.float32)
    gate_output = gate_output + adapter_scale * jnp.dot(expanded_gate, adapter_gate_weight.reshape(POLICY_VERSIONS * ADAPTER_RANK, -1), preferred_element_type=jnp.float32)
    up_output = jnp.dot(normed_input_rows, up_weight_matrix, preferred_element_type=jnp.float32)
    up_output = up_output + adapter_scale * jnp.dot(expanded_up, adapter_up_weight.reshape(POLICY_VERSIONS * ADAPTER_RANK, -1), preferred_element_type=jnp.float32)
    return (jax.nn.silu(gate_output) * up_output).astype(jnp.bfloat16)
```

```python
import functools

import jax
import jax.numpy as jnp
from jax import lax
from jax.experimental import pallas as pl
from jax.experimental.pallas import tpu as pltpu
from jax.sharding import PartitionSpec as P

ADAPTER_RANK = 64
POLICY_VERSIONS = 8
ROWS_DEV = 8
adapter_scale = 2.0

F32, BF16 = jnp.float32, jnp.bfloat16
MiB = 2**20
VM = pl.BlockSpec(memory_space=pltpu.VMEM)
HB = pl.BlockSpec(memory_space=pltpu.HBM)
LANE_BITS = ((4, 2, 1), (1, 4, 2))


def dot(a, b):
    return jnp.dot(a, b, preferred_element_type=F32)


def place():
    me = lax.axis_index("rep")
    return me // 2, lax.rem(me, 2)


def call(body, outs, ins, specs=None, scratch=(), vmem=2, bytes_=0, flops=0, alias=None, out_specs=None):
    return pl.pallas_call(
        body,
        out_shape=outs,
        in_specs=[VM] * len(ins) if specs is None else specs,
        out_specs=jax.tree.map(lambda _: VM, outs),
        scratch_shapes=list(scratch),
        input_output_aliases=alias or {},
        compiler_params=pltpu.CompilerParams(vmem_limit_bytes=int(vmem * MiB)),
        cost_estimate=pl.CostEstimate(flops=int(flops), bytes_accessed=int(bytes_), transcendentals=0),
    )(*ins)


def like(rows, cols, dtype=BF16):
    return jax.ShapeDtypeStruct((rows, cols), dtype)


def prep(x_ref, c_ref, m_ref, s_ref, o_ref):
    o_ref[...] = c_ref[...]
    _, core = place()
    for q in range(8):
        for lane, to_ref in ((core, m_ref), (1 - core, s_ref)):
            cols = pl.ds(pl.multiple_of((2 * q + lane) * 512, 512), 512)
            to_ref[:, q * 512 : q * 512 + 512] = x_ref[:, cols]


def pair(m_ref, r_ref, o_ref):
    _, core = place()
    mine, other = m_ref[...], r_ref[...]
    first = jnp.where(core == 0, mine, other)
    second = jnp.where(core == 0, other, mine)
    o_ref[...] = jnp.concatenate([first, second], axis=0)


def double(step, m_ref, r_ref, o_ref):
    chip, core = place()
    rows = m_ref.shape[0]
    bit = jnp.where(core == 0, lax.rem(chip // LANE_BITS[0][step], 2), lax.rem(chip // LANE_BITS[1][step], 2))
    o_ref[pl.ds(pl.multiple_of(bit * rows, rows), rows), :] = m_ref[...]
    o_ref[pl.ds(pl.multiple_of((1 - bit) * rows, rows), rows), :] = r_ref[...]


def settle(m_ref, r_ref, o_ref):
    chip, core = place()
    for lane, (b0, b1, b2) in enumerate(LANE_BITS):

        @pl.when(core == lane)
        def _(b0=b0, b1=b1, b2=b2):
            last = lax.rem(chip // b2, 2)
            for i in range(4):
                base = b0 * (i & 1) + b1 * (i >> 1)
                for ref, bit in ((m_ref, last), (r_ref, 1 - last)):
                    to = pl.multiple_of((base + b2 * bit) * 16, 16)
                    o_ref[pl.ds(to, 16), :] = ref[i * 16 : i * 16 + 16, :]


def versions(c_ref, o_ref):
    rows, reps = o_ref.shape[0], c_ref.shape[1]
    row = lax.broadcasted_iota(jnp.int32, (rows, reps), 0)
    holds = (row // ROWS_DEV == lax.broadcasted_iota(jnp.int32, (rows, reps), 1)).astype(F32)
    counts = lax.dot_general(holds, c_ref[...].astype(F32), (((1,), (1,)), ((), ())), preferred_element_type=F32)
    spot = lax.rem(lax.broadcasted_iota(jnp.int32, (rows, 1), 0), ROWS_DEV).astype(F32)
    running = jnp.zeros_like(spot)
    version = jnp.zeros((rows, 1), jnp.int32)
    for v in range(POLICY_VERSIONS):
        running = running + counts[:, v : v + 1]
        version = version + (running <= spot).astype(jnp.int32)
    o_ref[...] = jnp.broadcast_to(version, o_ref.shape)


def partial(x_ref, d_ref, v_ref, o_ref):
    chip, _ = place()
    x = x_ref[:, pl.ds(pl.multiple_of(chip * 512, 512), 512)]
    version = v_ref[...]
    total = jnp.zeros(o_ref.shape, F32)
    for v in range(POLICY_VERSIONS):
        total = total + jnp.where(version == v, dot(x, d_ref[v]), 0.0)
    o_ref[...] = total


def add(a_ref, b_ref, o_ref):
    o_ref[...] = a_ref[...] + b_ref[...]


HALF = 2


def copies_of(units, hbm_refs, to_refs, sem):
    _, core = place()
    copies = []
    for i, ((matrix, other, half), to_ref) in enumerate(zip(units, to_refs)):
        lane = 1 - core if other else core
        for k in range(HALF):
            row = pl.multiple_of((2 * (half * HALF + k) + lane) * 512, 512)
            copies.append(
                pltpu.make_async_copy(
                    hbm_refs[matrix].at[pl.ds(row, 512), :], to_ref.at[pl.ds(k * 512, 512), :], sem.at[i * HALF + k]
                )
            )
    return copies


def work(todo, xs, have, units, hbm, totals):
    rows, cols = 128, hbm[0].shape[1]
    done = sorted({m for m, _, _ in todo})
    used = sorted({o for _, o, _ in todo})
    old = [m for m in done if totals[m] is not None]
    nt, nu = len(todo), len(units)

    def body(*refs):
        refs = list(refs)

        def take(n):
            got, refs[:] = refs[:n], refs[n:]
            return got

        x_refs = dict(zip(used, take(len(used))))
        w_refs = take(nt)
        hbm_refs = take(2)
        old_refs = dict(zip(old, take(len(old))))
        new_refs = dict(zip(done, take(len(done))))
        to_refs = take(nu)
        copies = copies_of(units, hbm_refs, to_refs, refs[0]) if nu else []
        for c in copies:
            c.start()
        _, core = place()

        @pl.when(core >= 0)
        def _():
            for m in done:
                for n in range(0, cols, 256):
                    total = old_refs[m][:, n : n + 256] if m in old_refs else None
                    for (m2, other, half), w_ref in zip(todo, w_refs):
                        if m2 == m:
                            x = x_refs[other][:, half * HALF * 512 : (half + 1) * HALF * 512]
                            term = dot(x, w_ref[:, n : n + 256])
                            total = term if total is None else total + term
                    new_refs[m][:, n : n + 256] = total

        for c in copies:
            c.wait()

    ins = [xs[o] for o in used] + [have[t] for t in todo]
    specs = [VM] * len(ins) + [HB] * 2 + [VM] * len(old)
    ins += hbm
    alias = {len(ins) + i: done.index(m) for i, m in enumerate(old)}
    ins += [totals[m] for m in old]
    outs = [like(rows, cols, F32) for _ in done] + [like(HALF * 512, cols) for _ in units]
    got = call(
        body, outs, ins, specs, [pltpu.SemaphoreType.DMA((nu * HALF,))] if nu else [], vmem=4, alias=alias,
        bytes_=HALF * 512 * cols * 2 * max(nt, nu), flops=2 * rows * HALF * 512 * cols * nt,
    )
    for m, t in zip(done, got):
        totals[m] = t
    for unit, w in zip(units, got[len(done) :]):
        have[unit] = pltpu.with_memory_space_constraint(w, pltpu.VMEM)
    return got


def finish(tg_ref, tu_ref, s_ref, r_ref, v_ref, ag_ref, au_ref, o_ref):
    shrink = s_ref[...] + r_ref[...]
    turned = pltpu.roll(shrink, ADAPTER_RANK, 1)
    low = lax.broadcasted_iota(jnp.int32, shrink.shape, 1) < ADAPTER_RANK
    version = v_ref[...]
    half = (lax.broadcasted_iota(jnp.int32, shrink.shape, 1) >= ADAPTER_RANK).astype(jnp.int32)
    wide = []
    for twice in (jnp.where(low, shrink, turned), jnp.where(low, turned, shrink)):
        parts = [jnp.where(version == 2 * k + half, twice, 0.0).astype(BF16) for k in range(POLICY_VERSIONS // 2)]
        wide.append(jnp.concatenate(parts, axis=1))
    for n in range(0, o_ref.shape[1], 256):
        gate = tg_ref[:, n : n + 256] + adapter_scale * dot(wide[0], ag_ref[:, n : n + 256])
        up = tu_ref[:, n : n + 256] + adapter_scale * dot(wide[1], au_ref[:, n : n + 256])
        o_ref[:, n : n + 256] = (gate / (1.0 + jnp.exp(-gate)) * up).astype(BF16)


def cores(n):
    return [(i, i ^ 1) for i in range(n)]


def lanes(step):
    return [(2 * c + k, 2 * (c ^ LANE_BITS[k][step]) + k) for c in range(8) for k in range(2)]


def chips(bit):
    return [(i, i ^ (2 * bit)) for i in range(16)]


def permute(x, pairs):
    return lax.ppermute(x, "rep", pairs)


PLAN = (1, 4, 4)
AFTER = (3, 4, 0, 0)


def split(items, sizes):
    return [items[sum(sizes[:i]) : sum(sizes[: i + 1])] for i in range(len(sizes))]


def hold(*values):
    return lax.optimization_barrier(values)


def tuned(x, counts, g, u, down, ag, au):
    cols = g.shape[1]
    hbm = [pltpu.with_memory_space_constraint(w, pltpu.HBM) for w in (g, u)]
    rows = counts.shape[0] * ROWS_DEV
    order = [(m, o, h) for o in range(2) for h in range(8 // HALF) for m in range(2)]
    plan = split(order, PLAN)
    have, totals = {}, [None, None]
    mine, send, counts = call(prep, [like(8, 4096)] * 2 + [like(POLICY_VERSIONS, rows // ROWS_DEV, jnp.int32)], (x, counts.T))
    a = call(pair, like(16, 4096), (mine, permute(send, cores(16))))
    version = call(versions, like(rows, 128, jnp.int32), (counts,))
    for step in range(3):
        r = permute(a, lanes(step))
        work([], [], have, plan[step], hbm, totals)
        last = plan[step][-1]
        if step == 0:
            r, version, have[last] = hold(r, version, have[last])
        else:
            r, have[last] = hold(r, have[last])
        body = functools.partial(double, step) if step < 2 else settle
        a = call(body, like(a.shape[0] * 2, 4096), (a, r))
    other = permute(a, cores(16))
    xs = [a, other]
    part = call(partial, like(rows, 128, F32), (a, down, version))
    got = permute(part, cores(16))
    after = split(order[sum(PLAN) :], AFTER)
    for j in range(4):
        todo = order[4 * j : 4 * j + 4]
        work(todo, xs, have, after[j], hbm, totals)
        if j < 3:
            got, totals[0] = hold(got, totals[0])
            part = call(add, like(rows, 128, F32), (part, got))
            got = permute(part, chips((4, 2, 1)[j]))
    wide = POLICY_VERSIONS * ADAPTER_RANK
    return call(finish, like(rows, cols), (*totals, part, got, version, ag.reshape(wide, cols), au.reshape(wide, cols)), vmem=6)


def row_versions(counts):
    running = jnp.cumsum(counts, axis=1)
    place = jnp.arange(ROWS_DEV, dtype=jnp.int32)
    version = jnp.sum((running[:, None, :] <= place[None, :, None]).astype(jnp.int32), axis=2)
    return version.reshape(-1)


def spread_rank(onehot, factors):
    total_rows = factors.shape[0]
    widened = onehot[:, :, None] * factors.astype(jnp.float32)[:, None, :]
    return widened.reshape(total_rows, POLICY_VERSIONS * ADAPTER_RANK).astype(jnp.bfloat16)


def general(
    normed_input_rows,
    counts,
    gate_weight_matrix,
    up_weight_matrix,
    adapter_down_weight,
    adapter_gate_weight,
    adapter_up_weight,
):
    version = row_versions(counts)
    onehot_all = (version[:, None] == jnp.arange(POLICY_VERSIONS, dtype=jnp.int32)[None, :]).astype(
        jnp.float32
    )
    hidden_local = gate_weight_matrix.shape[1]
    feat_count = adapter_down_weight.shape[1]
    feat_start = lax.axis_index("rep") * feat_count
    piece = lax.all_gather(normed_input_rows, "rep", axis=0, tiled=True)
    feat_slice = lax.dynamic_slice_in_dim(piece, feat_start, feat_count, 1)
    every_version_output = jnp.einsum(
        "tj,bjo->tbo", feat_slice, adapter_down_weight, preferred_element_type=jnp.float32
    )
    partial_sum = jnp.sum(every_version_output * onehot_all[:, :, None], axis=1)
    base_gate = jnp.dot(piece, gate_weight_matrix, preferred_element_type=jnp.float32)
    base_up = jnp.dot(piece, up_weight_matrix, preferred_element_type=jnp.float32)
    combined_down = jnp.concatenate([base_gate, base_up, partial_sum], axis=1)
    shrink = lax.psum(combined_down[:, 2 * hidden_local :], "rep").astype(jnp.bfloat16)
    expanded_gate = spread_rank(onehot_all, shrink[:, :ADAPTER_RANK])
    expanded_up = spread_rank(onehot_all, shrink[:, ADAPTER_RANK:])
    gate_output = combined_down[:, :hidden_local] + adapter_scale * jnp.dot(
        expanded_gate,
        adapter_gate_weight.reshape(POLICY_VERSIONS * ADAPTER_RANK, hidden_local),
        preferred_element_type=jnp.float32,
    )
    up_output = combined_down[:, hidden_local : 2 * hidden_local] + adapter_scale * jnp.dot(
        expanded_up,
        adapter_up_weight.reshape(POLICY_VERSIONS * ADAPTER_RANK, hidden_local),
        preferred_element_type=jnp.float32,
    )
    return (jax.nn.silu(gate_output) * up_output).astype(jnp.bfloat16)


def solution(mesh):
    placed = (
        P(("groups", "rep"), None),
        P("groups", None),
        P(None, "rep"),
        P(None, "rep"),
        P("groups", "rep", None),
        P("groups", None, "rep"),
        P("groups", None, "rep"),
    )
    local = tuned if mesh.shape["rep"] == 16 else general
    return jax.shard_map(local, mesh=mesh, in_specs=placed, out_specs=P("groups", "rep"), check_vma=False)
```

```python
import functools

import jax
import jax.numpy as jnp
from jax import lax
from jax.experimental import pallas as pl
from jax.experimental.pallas import tpu as pltpu
from jax.sharding import PartitionSpec as P

ADAPTER_RANK = 64
POLICY_VERSIONS = 8
ROWS_DEV = 8
adapter_scale = 2.0

F32, BF16 = jnp.float32, jnp.bfloat16
MiB = 2**20
VM = pl.BlockSpec(memory_space=pltpu.VMEM)
HB = pl.BlockSpec(memory_space=pltpu.HBM)

LANE_BITS = ((4, 2, 1), (1, 4, 2))
SUM_BITS = (1, 2, 4)
UNIT = 1024
EARLY = (1, 4, 5)
LATE = (2, 2, 2, 0)


def dot(a, b):
    return jnp.dot(a, b, preferred_element_type=F32)


def place():
    me = lax.axis_index("rep")
    return me // 2, lax.rem(me, 2)


def chip_of(core, spot):
    return sum(bit * ((spot >> k) & 1) for k, bit in enumerate(LANE_BITS[core]))


def like(shape, dtype=BF16):
    return jax.ShapeDtypeStruct(shape, dtype)


def call(body, outs, ins, specs=None, scratch=(), vmem=2, bytes_=0, flops=0, alias=None):
    return pl.pallas_call(
        body,
        out_shape=outs,
        in_specs=[VM] * len(ins) if specs is None else specs,
        out_specs=jax.tree.map(lambda _: VM, outs),
        scratch_shapes=list(scratch),
        input_output_aliases=alias or {},
        compiler_params=pltpu.CompilerParams(vmem_limit_bytes=int(vmem * MiB)),
        cost_estimate=pl.CostEstimate(flops=int(flops), bytes_accessed=int(bytes_), transcendentals=0),
    )(*ins)


def double(step, m_ref, r_ref, o_ref):
    chip, core = place()
    rows = m_ref.shape[0]
    bit = jnp.where(core == 0, lax.rem(chip // LANE_BITS[0][step], 2), lax.rem(chip // LANE_BITS[1][step], 2))
    if step == 0:
        mine, other = m_ref[...], r_ref[...]
        first = jnp.where(bit == 0, mine, other)
        second = jnp.where(bit == 0, other, mine)
        o_ref[...] = jnp.concatenate([first, second], axis=0)
    else:
        o_ref[pl.ds(pl.multiple_of(bit * rows, rows), rows), :] = m_ref[...]
        o_ref[pl.ds(pl.multiple_of((1 - bit) * rows, rows), rows), :] = r_ref[...]


def join(m_ref, r_ref, o_ref):
    _, core = place()
    rows = m_ref.shape[0]
    o_ref[pl.ds(pl.multiple_of(core * rows, rows), rows), :] = m_ref[...]
    o_ref[pl.ds(pl.multiple_of((1 - core) * rows, rows), rows), :] = r_ref[...]


def versions(c_ref, o_ref):
    rows, reps = o_ref.shape[0], c_ref.shape[1]
    row = lax.broadcasted_iota(jnp.int32, (rows, reps), 0)
    group = row // ROWS_DEV
    spot, core = lax.rem(group, 8), group // 8
    chip = jnp.where(core == 0, chip_of(0, spot), chip_of(1, spot))
    holds = (2 * chip + core == lax.broadcasted_iota(jnp.int32, (rows, reps), 1)).astype(F32)
    counts = lax.dot_general(holds, c_ref[...].astype(F32), (((1,), (1,)), ((), ())), preferred_element_type=F32)
    spot = lax.rem(lax.broadcasted_iota(jnp.int32, (rows, 1), 0), ROWS_DEV).astype(F32)
    running = jnp.zeros_like(spot)
    version = jnp.zeros((rows, 1), jnp.int32)
    for v in range(POLICY_VERSIONS):
        running = running + counts[:, v : v + 1]
        version = version + (running <= spot).astype(jnp.int32)
    o_ref[...] = jnp.broadcast_to(version, o_ref.shape)


def partial(x_ref, d_ref, e_ref, v_ref, o_ref):
    chip, core = place()
    feats = d_ref.shape[1]
    mine = x_ref[:, pl.ds(pl.multiple_of((2 * chip + core) * feats, feats), feats)]
    other = x_ref[:, pl.ds(pl.multiple_of((2 * chip + 1 - core) * feats, feats), feats)]
    rows = x_ref.shape[0]
    version = v_ref[pl.ds(pl.multiple_of(core * rows, rows), rows), :]
    total = jnp.zeros(o_ref.shape, F32)
    for v in range(POLICY_VERSIONS):
        total = total + jnp.where(version == v, dot(mine, d_ref[v]) + dot(other, e_ref[v]), 0.0)
    o_ref[...] = total


def add(*refs):
    total = refs[0][...]
    for ref in refs[1:-1]:
        total = total + ref[...]
    refs[-1][...] = total


def finish(tg_ref, tu_ref, s_ref, r_ref, v_ref, ag_ref, au_ref, o_ref):
    _, core = place()
    mine, other = s_ref[...], r_ref[...]
    shrink = jnp.concatenate([jnp.where(core == 0, mine, other), jnp.where(core == 0, other, mine)], axis=0)
    turned = pltpu.roll(shrink, ADAPTER_RANK, 1)
    column = lax.broadcasted_iota(jnp.int32, shrink.shape, 1)
    low = column < ADAPTER_RANK
    version = v_ref[...]
    half = (column >= ADAPTER_RANK).astype(jnp.int32)
    wide = []
    for twice in (jnp.where(low, shrink, turned), jnp.where(low, turned, shrink)):
        parts = [jnp.where(version == 2 * k + half, twice, 0.0).astype(BF16) for k in range(POLICY_VERSIONS // 2)]
        wide.append(jnp.concatenate(parts, axis=1))
    groups = shrink.shape[0] // ROWS_DEV
    where = {}
    for core_ in range(2):
        for spot in range(groups // 2):
            where[2 * chip_of(core_, spot) + core_] = (core_ * (groups // 2) + spot) * ROWS_DEV
    for n in range(0, o_ref.shape[1], 256):
        gate = tg_ref[:, n : n + 256] + adapter_scale * dot(wide[0], ag_ref[:, n : n + 256])
        up = tu_ref[:, n : n + 256] + adapter_scale * dot(wide[1], au_ref[:, n : n + 256])
        hidden = gate / (1.0 + jnp.exp(-gate)) * up
        for r in range(0, groups, 2):
            two = [hidden[where[k] : where[k] + ROWS_DEV] for k in (r, r + 1)]
            o_ref[r * ROWS_DEV : (r + 2) * ROWS_DEV, n : n + 256] = jnp.concatenate(two, axis=0).astype(BF16)


def work(todo, x, have, units, hbm, totals):
    cols = hbm[0].shape[1]
    done = sorted({m for m, _ in todo})
    old = [m for m in done if totals[m] is not None]
    nt, nu = len(todo), len(units)

    def body(*refs):
        refs = list(refs)

        def take(n):
            got, refs[:] = refs[:n], refs[n:]
            return got

        x_refs, w_refs, hbm_refs = take(1 if nt else 0), take(nt), take(2)
        old_refs, new_refs = dict(zip(old, take(len(old)))), dict(zip(done, take(len(done))))
        copies = [
            pltpu.make_async_copy(
                hbm_refs[m].at[pl.ds(k * UNIT + h * UNIT // 2, UNIT // 2), :], to_ref.at[pl.ds(h * UNIT // 2, UNIT // 2), :], refs[nu].at[2 * i + h]
            )
            for i, ((m, k), to_ref) in enumerate(zip(units, refs[:nu]))
            for h in range(2)
        ]
        for c in copies:
            c.start()

        @pl.when(lax.axis_index("rep") >= 0)
        def _():
            for m in done:
                for n in range(0, cols, 256):
                    total = old_refs[m][:, n : n + 256] if m in old_refs else None
                    for (m2, k), w_ref in zip(todo, w_refs):
                        if m2 == m:
                            term = dot(x_refs[0][:, k * UNIT : (k + 1) * UNIT], w_ref[:, n : n + 256])
                            total = term if total is None else total + term
                    new_refs[m][:, n : n + 256] = total

        for c in copies:
            c.wait()

    ins = ([x] if nt else []) + [have[t] for t in todo]
    specs = [VM] * len(ins) + [HB] * 2 + [VM] * len(old)
    ins += hbm
    alias = {len(ins) + i: done.index(m) for i, m in enumerate(old)}
    ins += [totals[m] for m in old]
    rows = x.shape[0] if nt else 0
    outs = [like((rows, cols), F32) for _ in done] + [like((UNIT, cols)) for _ in units]
    got = call(
        body, outs, ins, specs, [pltpu.SemaphoreType.DMA((2 * nu,))] if nu else [], vmem=4, alias=alias,
        bytes_=UNIT * cols * 2 * max(nt, nu), flops=2 * rows * UNIT * cols * nt,
    )
    for m, t in zip(done, got):
        totals[m] = t
    for unit, w in zip(units, got[len(done) :]):
        have[unit] = pltpu.with_memory_space_constraint(w, pltpu.VMEM)


def cores():
    return [(i, i ^ 1) for i in range(16)]


def lanes(step):
    return [(2 * c + k, 2 * (c ^ LANE_BITS[k][step]) + k) for c in range(8) for k in range(2)]


def chips(bits):
    return [(i, i ^ (2 * bits)) for i in range(16)]


def permute(x, pairs):
    return lax.ppermute(x, "rep", pairs)


def split(items, sizes):
    return [items[sum(sizes[:i]) : sum(sizes[: i + 1])] for i in range(len(sizes))]


def hold(*values):
    return lax.optimization_barrier(values)


def tuned(x, counts, g, u, down, ag, au):
    feats, cols = g.shape
    hbm = [pltpu.with_memory_space_constraint(w, pltpu.HBM) for w in (g, u)]
    rows = counts.shape[0] * ROWS_DEV
    order = [(m, k) for k in range(feats // UNIT) for m in range(2)]
    early = split(order, EARLY)
    late = split(order[sum(EARLY) :], LATE)
    have, totals = {}, [None, None]
    a = x
    for step in range(3):
        r = permute(a, lanes(step))
        if step == 0:
            e = permute(down, cores())
            version = call(versions, like((rows, 128), jnp.int32), (counts.T,))
        work([], None, have, early[step], hbm, totals)
        last = early[step][-1]
        if step == 0:
            r, version, have[last] = hold(r, version, have[last])
        else:
            r, have[last] = hold(r, have[last])
        a = call(functools.partial(double, step), like((a.shape[0] * 2, feats)), (a, r))
    other = permute(a, cores())
    part = call(partial, like((rows // 2, 128), F32), (a, down, e, version))
    got = permute(part, chips(SUM_BITS[0]))
    x = call(join, like((rows, feats)), (a, other))
    per = len(order) // 4
    for j in range(4):
        work(order[per * j : per * (j + 1)], x, have, late[j], hbm, totals)
        if j < 3:
            got, totals[0] = hold(got, totals[0])
            part = call(add, like((rows // 2, 128), F32), (part, got))
            got = permute(part, chips(SUM_BITS[j + 1]) if j < 2 else cores())
    wide = POLICY_VERSIONS * ADAPTER_RANK
    return call(
        finish, like((rows, cols)), (*totals, part, got, version, ag.reshape(wide, cols), au.reshape(wide, cols)), vmem=6
    )


def row_versions(counts):
    running = jnp.cumsum(counts, axis=1)
    place = jnp.arange(ROWS_DEV, dtype=jnp.int32)
    version = jnp.sum((running[:, None, :] <= place[None, :, None]).astype(jnp.int32), axis=2)
    return version.reshape(-1)


def spread_rank(onehot, factors):
    total_rows = factors.shape[0]
    widened = onehot[:, :, None] * factors.astype(jnp.float32)[:, None, :]
    return widened.reshape(total_rows, POLICY_VERSIONS * ADAPTER_RANK).astype(jnp.bfloat16)


def general(
    normed_input_rows,
    counts,
    gate_weight_matrix,
    up_weight_matrix,
    adapter_down_weight,
    adapter_gate_weight,
    adapter_up_weight,
):
    version = row_versions(counts)
    onehot_all = (version[:, None] == jnp.arange(POLICY_VERSIONS, dtype=jnp.int32)[None, :]).astype(
        jnp.float32
    )
    hidden_local = gate_weight_matrix.shape[1]
    feat_count = adapter_down_weight.shape[1]
    feat_start = lax.axis_index("rep") * feat_count
    piece = lax.all_gather(normed_input_rows, "rep", axis=0, tiled=True)
    feat_slice = lax.dynamic_slice_in_dim(piece, feat_start, feat_count, 1)
    every_version_output = jnp.einsum(
        "tj,bjo->tbo", feat_slice, adapter_down_weight, preferred_element_type=jnp.float32
    )
    partial_sum = jnp.sum(every_version_output * onehot_all[:, :, None], axis=1)
    base_gate = jnp.dot(piece, gate_weight_matrix, preferred_element_type=jnp.float32)
    base_up = jnp.dot(piece, up_weight_matrix, preferred_element_type=jnp.float32)
    combined_down = jnp.concatenate([base_gate, base_up, partial_sum], axis=1)
    shrink = lax.psum(combined_down[:, 2 * hidden_local :], "rep").astype(jnp.bfloat16)
    expanded_gate = spread_rank(onehot_all, shrink[:, :ADAPTER_RANK])
    expanded_up = spread_rank(onehot_all, shrink[:, ADAPTER_RANK:])
    gate_output = combined_down[:, :hidden_local] + adapter_scale * jnp.dot(
        expanded_gate,
        adapter_gate_weight.reshape(POLICY_VERSIONS * ADAPTER_RANK, hidden_local),
        preferred_element_type=jnp.float32,
    )
    up_output = combined_down[:, hidden_local : 2 * hidden_local] + adapter_scale * jnp.dot(
        expanded_up,
        adapter_up_weight.reshape(POLICY_VERSIONS * ADAPTER_RANK, hidden_local),
        preferred_element_type=jnp.float32,
    )
    return (jax.nn.silu(gate_output) * up_output).astype(jnp.bfloat16)


def solution(mesh):
    placed = (
        P(("groups", "rep"), None),
        P("groups", None),
        P(None, "rep"),
        P(None, "rep"),
        P("groups", "rep", None),
        P("groups", None, "rep"),
        P("groups", None, "rep"),
    )
    local = tuned if mesh.shape["rep"] == 16 else general
    return jax.shard_map(local, mesh=mesh, in_specs=placed, out_specs=P("groups", "rep"), check_vma=False)
```

```python
import functools

import jax
import jax.numpy as jnp
from jax import lax
from jax.experimental import pallas as pl
from jax.experimental.pallas import tpu as pltpu
from jax.sharding import PartitionSpec as P

ADAPTER_RANK = 64
POLICY_VERSIONS = 8
ROWS_DEV = 8
adapter_scale = 2.0

F32, BF16 = jnp.float32, jnp.bfloat16
MiB = 2**20
VM = pl.BlockSpec(memory_space=pltpu.VMEM)
HB = pl.BlockSpec(memory_space=pltpu.HBM)

LANE_BITS = ((1, 4, 2), (4, 2, 1))
SUM_BITS = (4, 2, 1)
UNIT = 1024
COST = 1000
CUTS = 2
EARLY = (2, 4, 5)
TURNS = (4, 4, 4, 2, 2)
MID = 0
LATE = (2, 2, 1, 0)
MAPS = 2
ROOM = (1, 2, 3)


def dot(a, b):
    return jnp.dot(a, b, preferred_element_type=F32)


def place():
    me = lax.axis_index("rep")
    return me // 2, lax.rem(me, 2)


def chip_of(core, spot):
    return sum(bit * ((spot >> k) & 1) for k, bit in enumerate(LANE_BITS[core]))


def like(shape, dtype=BF16):
    return jax.ShapeDtypeStruct(shape, dtype)


def call(body, outs, ins, specs=None, scratch=(), vmem=None, bytes_=0, flops=0, alias=None):
    return pl.pallas_call(
        body,
        out_shape=outs,
        in_specs=[VM] * len(ins) if specs is None else specs,
        out_specs=jax.tree.map(lambda _: VM, outs),
        scratch_shapes=list(scratch),
        input_output_aliases=alias or {},
        compiler_params=pltpu.CompilerParams(vmem_limit_bytes=int((vmem or ROOM[0]) * MiB)),
        cost_estimate=pl.CostEstimate(flops=int(flops), bytes_accessed=int(bytes_), transcendentals=0),
    )(*ins)


def double(step, m_ref, r_ref, o_ref):
    chip, core = place()
    rows = m_ref.shape[0]
    bit = jnp.where(core == 0, lax.rem(chip // LANE_BITS[0][step], 2), lax.rem(chip // LANE_BITS[1][step], 2))
    if step == 0:
        mine, other = m_ref[...], r_ref[...]
        first = jnp.where(bit == 0, mine, other)
        second = jnp.where(bit == 0, other, mine)
        o_ref[...] = jnp.concatenate([first, second], axis=0)
    else:
        o_ref[pl.ds(pl.multiple_of(bit * rows, rows), rows), :] = m_ref[...]
        o_ref[pl.ds(pl.multiple_of((1 - bit) * rows, rows), rows), :] = r_ref[...]


def join(m_ref, r_ref, o_ref):
    _, core = place()
    rows = m_ref.shape[0]
    o_ref[pl.ds(pl.multiple_of(core * rows, rows), rows), :] = m_ref[...]
    o_ref[pl.ds(pl.multiple_of((1 - core) * rows, rows), rows), :] = r_ref[...]


def versions(c_ref, o_ref):
    rows, reps = o_ref.shape[0], c_ref.shape[1]
    row = lax.broadcasted_iota(jnp.int32, (rows, reps), 0)
    group = row // ROWS_DEV
    spot, core = lax.rem(group, 8), group // 8
    chip = jnp.where(core == 0, chip_of(0, spot), chip_of(1, spot))
    holds = (2 * chip + core == lax.broadcasted_iota(jnp.int32, (rows, reps), 1)).astype(F32)
    counts = lax.dot_general(holds, c_ref[...].astype(F32), (((1,), (1,)), ((), ())), preferred_element_type=F32)
    spot = lax.rem(lax.broadcasted_iota(jnp.int32, (rows, 1), 0), ROWS_DEV).astype(F32)
    running = jnp.zeros_like(spot)
    version = jnp.zeros((rows, 1), jnp.int32)
    for v in range(POLICY_VERSIONS):
        running = running + counts[:, v : v + 1]
        version = version + (running <= spot).astype(jnp.int32)
    o_ref[...] = jnp.broadcast_to(version, o_ref.shape)


def partial(x_ref, d_ref, e_ref, v_ref, o_ref):
    chip, core = place()
    feats = d_ref.shape[1]
    mine = x_ref[:, pl.ds(pl.multiple_of((2 * chip + core) * feats, feats), feats)]
    other = x_ref[:, pl.ds(pl.multiple_of((2 * chip + 1 - core) * feats, feats), feats)]
    rows = x_ref.shape[0]
    version = v_ref[pl.ds(pl.multiple_of(core * rows, rows), rows), :]
    total = jnp.zeros(o_ref.shape, F32)
    for v in range(POLICY_VERSIONS):
        total = total + jnp.where(version == v, dot(mine, d_ref[v]) + dot(other, e_ref[v]), 0.0)
    o_ref[...] = total


def add(*refs):
    total = refs[0][...]
    for ref in refs[1:-1]:
        total = total + ref[...]
    refs[-1][...] = total


def finish(todo, x, have, totals, part, got, version, ag, au):
    rows, cols = totals[0].shape
    nt = len(todo)

    def body(x_ref, *refs):
        w_refs, (tg_ref, tu_ref, s_ref, r_ref, v_ref, ag_ref, au_ref, o_ref) = refs[:nt], refs[nt:]
        _, core = place()
        mine, other = s_ref[...], r_ref[...]
        shrink = jnp.concatenate([jnp.where(core == 0, mine, other), jnp.where(core == 0, other, mine)], axis=0)
        turned = pltpu.roll(shrink, ADAPTER_RANK, 1)
        column = lax.broadcasted_iota(jnp.int32, shrink.shape, 1)
        low = column < ADAPTER_RANK
        version = v_ref[...]
        half = (column >= ADAPTER_RANK).astype(jnp.int32)
        wide = []
        for twice in (jnp.where(low, shrink, turned), jnp.where(low, turned, shrink)):
            parts = [jnp.where(version == 2 * k + half, twice, 0.0).astype(BF16) for k in range(POLICY_VERSIONS // 2)]
            wide.append(jnp.concatenate(parts, axis=1))
        groups = rows // ROWS_DEV
        where = {}
        for core_ in range(2):
            for spot in range(groups // 2):
                where[2 * chip_of(core_, spot) + core_] = (core_ * (groups // 2) + spot) * ROWS_DEV
        for n in range(0, cols, 256):
            both = []
            for m, (t_ref, a_ref) in enumerate(((tg_ref, ag_ref), (tu_ref, au_ref))):
                total = t_ref[:, n : n + 256]
                for (m2, k), w_ref in zip(todo, w_refs):
                    if m2 == m:
                        total = total + dot(x_ref[:, k * UNIT : (k + 1) * UNIT], w_ref[:, n : n + 256])
                both.append(total + adapter_scale * dot(wide[m], a_ref[:, n : n + 256]))
            gate, up = both
            hidden = gate / (1.0 + jnp.exp(-gate)) * up
            for r in range(0, groups, 2):
                two = [hidden[where[k] : where[k] + ROWS_DEV] for k in (r, r + 1)]
                o_ref[r * ROWS_DEV : (r + 2) * ROWS_DEV, n : n + 256] = jnp.concatenate(two, axis=0).astype(BF16)

    ins = (x, *[have[t] for t in todo], *totals, part, got, version, ag, au)
    return call(body, like((rows, cols)), ins, vmem=ROOM[2])


def work(todo, x, have, units, hbm, totals, counts=None, maps=(), after=None):
    cols = hbm[0].shape[1]
    done = sorted({m for m, _ in todo})
    old = [m for m in done if totals[m] is not None]
    nt, nu = len(todo), len(units)

    def body(*refs):
        refs = list(refs)

        def take(n):
            got, refs[:] = refs[:n], refs[n:]
            return got

        take(1 if after is not None else 0)
        c_refs, map_refs = take(1 if counts is not None else 0), take(len(maps))
        x_refs, w_refs, hbm_refs = take(1 if nt else 0), take(nt), take(2)
        old_refs, new_refs = dict(zip(old, take(len(old)))), dict(zip(done, take(len(done))))
        to_refs, v_refs, got_refs = take(nu), take(len(c_refs)), take(len(maps))
        if c_refs:
            small = pltpu.make_async_copy(c_refs[0], refs[1], refs[2])
            small.start()
        copies = [
            pltpu.make_async_copy(
                hbm_refs[m].at[pl.ds(k * UNIT + h * UNIT // CUTS, UNIT // CUTS), :],
                to_ref.at[pl.ds(h * UNIT // CUTS, UNIT // CUTS), :],
                refs[0].at[CUTS * i + h],
            )
            for i, ((m, k), to_ref) in enumerate(zip(units, to_refs))
            for h in range(CUTS)
        ]
        copies += [pltpu.make_async_copy(f, t, refs[0].at[CUTS * nu + i]) for i, (f, t) in enumerate(zip(map_refs, got_refs))]
        for c in copies:
            c.start()
        if c_refs:
            small.wait()
            versions(refs[1], v_refs[0])

        @pl.when(lax.axis_index("rep") >= 0)
        def _():
            for m in done:
                for n in range(0, cols, 256):
                    total = old_refs[m][:, n : n + 256] if m in old_refs else None
                    for (m2, k), w_ref in zip(todo, w_refs):
                        if m2 == m:
                            term = dot(x_refs[0][:, k * UNIT : (k + 1) * UNIT], w_ref[:, n : n + 256])
                            total = term if total is None else total + term
                    new_refs[m][:, n : n + 256] = total

        for c in copies:
            c.wait()

    ins = ([x] if nt else []) + [have[t] for t in todo]
    specs = [VM] * len(ins) + [HB] * 2 + [VM] * len(old)
    ncopy = CUTS * nu + len(maps)
    scratch = [pltpu.SemaphoreType.DMA((ncopy,))] if ncopy else []
    ins, specs = [*maps, *ins], [HB] * len(maps) + specs
    if counts is not None:
        ins, specs = [counts, *ins], [HB, *specs]
        scratch += [pltpu.VMEM(counts.shape, counts.dtype), pltpu.SemaphoreType.DMA]
    if after is not None:
        ins, specs = [after, *ins], [VM, *specs]
    ins += hbm
    alias = {len(ins) + i: done.index(m) for i, m in enumerate(old)}
    ins += [totals[m] for m in old]
    rows = x.shape[0] if nt else 0
    outs = [like((rows, cols), F32) for _ in done] + [like((UNIT, cols)) for _ in units]
    if counts is not None:
        outs.append(like((counts.shape[1] * ROWS_DEV, 128), jnp.int32))
    outs += [like(f.shape) for f in maps]
    got = call(
        body, outs, ins, specs, scratch, vmem=ROOM[1], alias=alias,
        bytes_=COST,
    )
    for m, t in zip(done, got):
        totals[m] = t
    for unit, w in zip(units, got[len(done) :]):
        have[unit] = pltpu.with_memory_space_constraint(w, pltpu.VMEM)
    return got[len(done) + nu :]


def cores():
    return [(i, i ^ 1) for i in range(16)]


def lanes(step):
    return [(2 * c + k, 2 * (c ^ LANE_BITS[k][step]) + k) for c in range(8) for k in range(2)]


def chips(bits):
    return [(i, i ^ (2 * bits)) for i in range(16)]


def permute(x, pairs):
    return lax.ppermute(x, "rep", pairs)


def split(items, sizes):
    return [items[sum(sizes[:i]) : sum(sizes[: i + 1])] for i in range(len(sizes))]


def hold(*values):
    return lax.optimization_barrier(values)


def tuned(x, counts, g, u, down, ag, au):
    feats, cols = g.shape
    hbm = [pltpu.with_memory_space_constraint(w, pltpu.HBM) for w in (g, u)]
    rows = counts.shape[0] * ROWS_DEV
    order = [(m, k) for k in range(feats // UNIT) for m in range(2)]
    early = split(order, EARLY)
    late = split(order[sum(EARLY) + MID :], LATE)
    have, totals = {}, [None, None]
    a = x
    for step in range(3):
        r = permute(a, lanes(step))
        if step == 0:
            e = permute(down, cores())
            (version,) = work([], None, have, early[step], hbm, totals, pltpu.with_memory_space_constraint(counts.T, pltpu.HBM))
        else:
            work([], None, have, early[step], hbm, totals)
        last = early[step][-1]
        if step == 0:
            r, e, version, have[last] = hold(r, e, version, have[last])
        else:
            r, have[last] = hold(r, have[last])
        a = call(functools.partial(double, step), like((a.shape[0] * 2, feats)), (a, r))
    other = permute(a, cores())
    part = call(partial, like((rows // 2, 128), F32), (a, down, e, version))
    got = permute(part, chips(SUM_BITS[0]))
    if MID:
        last = order[sum(EARLY) + MID - 1]
        work([], None, have, order[sum(EARLY) :][:MID], hbm, totals, after=part)
        other, have[last] = hold(other, have[last])
    x = call(join, like((rows, feats)), (a, other))
    turns = split(order, TURNS)
    wide = POLICY_VERSIONS * ADAPTER_RANK
    maps = [pltpu.with_memory_space_constraint(w.reshape(wide, cols), pltpu.HBM) for w in (ag, au)]
    for j in range(4):
        fetched = work(turns[j], x, have, late[j], hbm, totals, maps=maps if j == MAPS else ())
        if j == MAPS:
            maps = [pltpu.with_memory_space_constraint(w, pltpu.VMEM) for w in fetched]
        if j < 3:
            got, totals[0] = hold(got, totals[0])
            part = call(add, like((rows // 2, 128), F32), (part, got))
            got = permute(part, chips(SUM_BITS[j + 1]) if j < 2 else cores())
    return finish(turns[4], x, have, totals, part, got, version, *maps)


def row_versions(counts):
    running = jnp.cumsum(counts, axis=1)
    place = jnp.arange(ROWS_DEV, dtype=jnp.int32)
    version = jnp.sum((running[:, None, :] <= place[None, :, None]).astype(jnp.int32), axis=2)
    return version.reshape(-1)


def spread_rank(onehot, factors):
    total_rows = factors.shape[0]
    widened = onehot[:, :, None] * factors.astype(jnp.float32)[:, None, :]
    return widened.reshape(total_rows, POLICY_VERSIONS * ADAPTER_RANK).astype(jnp.bfloat16)


def general(
    normed_input_rows,
    counts,
    gate_weight_matrix,
    up_weight_matrix,
    adapter_down_weight,
    adapter_gate_weight,
    adapter_up_weight,
):
    version = row_versions(counts)
    onehot_all = (version[:, None] == jnp.arange(POLICY_VERSIONS, dtype=jnp.int32)[None, :]).astype(
        jnp.float32
    )
    hidden_local = gate_weight_matrix.shape[1]
    feat_count = adapter_down_weight.shape[1]
    feat_start = lax.axis_index("rep") * feat_count
    piece = lax.all_gather(normed_input_rows, "rep", axis=0, tiled=True)
    feat_slice = lax.dynamic_slice_in_dim(piece, feat_start, feat_count, 1)
    every_version_output = jnp.einsum(
        "tj,bjo->tbo", feat_slice, adapter_down_weight, preferred_element_type=jnp.float32
    )
    partial_sum = jnp.sum(every_version_output * onehot_all[:, :, None], axis=1)
    base_gate = jnp.dot(piece, gate_weight_matrix, preferred_element_type=jnp.float32)
    base_up = jnp.dot(piece, up_weight_matrix, preferred_element_type=jnp.float32)
    combined_down = jnp.concatenate([base_gate, base_up, partial_sum], axis=1)
    shrink = lax.psum(combined_down[:, 2 * hidden_local :], "rep").astype(jnp.bfloat16)
    expanded_gate = spread_rank(onehot_all, shrink[:, :ADAPTER_RANK])
    expanded_up = spread_rank(onehot_all, shrink[:, ADAPTER_RANK:])
    gate_output = combined_down[:, :hidden_local] + adapter_scale * jnp.dot(
        expanded_gate,
        adapter_gate_weight.reshape(POLICY_VERSIONS * ADAPTER_RANK, hidden_local),
        preferred_element_type=jnp.float32,
    )
    up_output = combined_down[:, hidden_local : 2 * hidden_local] + adapter_scale * jnp.dot(
        expanded_up,
        adapter_up_weight.reshape(POLICY_VERSIONS * ADAPTER_RANK, hidden_local),
        preferred_element_type=jnp.float32,
    )
    return (jax.nn.silu(gate_output) * up_output).astype(jnp.bfloat16)


def solution(mesh):
    placed = (
        P(("groups", "rep"), None),
        P("groups", None),
        P(None, "rep"),
        P(None, "rep"),
        P("groups", "rep", None),
        P("groups", None, "rep"),
        P("groups", None, "rep"),
    )
    local = tuned if mesh.shape["rep"] == 16 else general
    return jax.shard_map(local, mesh=mesh, in_specs=placed, out_specs=P("groups", "rep"), check_vma=False)
```

```python
import functools

import jax
import jax.numpy as jnp
from jax import lax
from jax.experimental import pallas as pl
from jax.experimental.pallas import tpu as pltpu
from jax.sharding import PartitionSpec as P

ADAPTER_RANK = 64
POLICY_VERSIONS = 8
ROWS_DEV = 8
adapter_scale = 2.0

F32, BF16 = jnp.float32, jnp.bfloat16
MiB = 2**20
VM = pl.BlockSpec(memory_space=pltpu.VMEM)
HB = pl.BlockSpec(memory_space=pltpu.HBM)

LANE_BITS = ((1, 4, 2), (4, 2, 1))
SUM_BITS = (4, 2, 1)
UNIT = 1024
COST = 1000
CUTS = 1
EARLY = (2, 4, 5)
TURNS = (4, 4, 4, 2, 2)
MID = 0
LATE = (1, 2, 2, 0)
MAPS = 3
ROOM = (1, 2, 3)


def dot(a, b):
    return jnp.dot(a, b, preferred_element_type=F32)


def place():
    me = lax.axis_index("rep")
    return me // 2, lax.rem(me, 2)


def chip_of(core, spot):
    return sum(bit * ((spot >> k) & 1) for k, bit in enumerate(LANE_BITS[core]))


def like(shape, dtype=BF16):
    return jax.ShapeDtypeStruct(shape, dtype)


def call(body, outs, ins, specs=None, scratch=(), vmem=None, bytes_=0, flops=0, alias=None):
    return pl.pallas_call(
        body,
        out_shape=outs,
        in_specs=[VM] * len(ins) if specs is None else specs,
        out_specs=jax.tree.map(lambda _: VM, outs),
        scratch_shapes=list(scratch),
        input_output_aliases=alias or {},
        compiler_params=pltpu.CompilerParams(vmem_limit_bytes=int((vmem or ROOM[0]) * MiB)),
        cost_estimate=pl.CostEstimate(flops=int(flops), bytes_accessed=int(bytes_), transcendentals=0),
    )(*ins)


def double(step, m_ref, r_ref, o_ref):
    chip, core = place()
    rows = m_ref.shape[0]
    bit = jnp.where(core == 0, lax.rem(chip // LANE_BITS[0][step], 2), lax.rem(chip // LANE_BITS[1][step], 2))
    if step == 0:
        mine, other = m_ref[...], r_ref[...]
        first = jnp.where(bit == 0, mine, other)
        second = jnp.where(bit == 0, other, mine)
        o_ref[...] = jnp.concatenate([first, second], axis=0)
    else:
        o_ref[pl.ds(pl.multiple_of(bit * rows, rows), rows), :] = m_ref[...]
        o_ref[pl.ds(pl.multiple_of((1 - bit) * rows, rows), rows), :] = r_ref[...]


def join(m_ref, a_ref, r_ref, o_ref):
    chip, core = place()
    rows, part = m_ref.shape[0], a_ref.shape[0]
    o_ref[pl.ds(pl.multiple_of(core * rows, rows), rows), :] = m_ref[...]
    bit = jnp.where(core == 0, lax.rem(chip // LANE_BITS[1][2], 2), lax.rem(chip // LANE_BITS[0][2], 2))
    base = (1 - core) * rows
    o_ref[pl.ds(pl.multiple_of(base + bit * part, part), part), :] = a_ref[...]
    o_ref[pl.ds(pl.multiple_of(base + (1 - bit) * part, part), part), :] = r_ref[...]


def versions(c_ref, o_ref):
    rows, reps = o_ref.shape[0], c_ref.shape[1]
    row = lax.broadcasted_iota(jnp.int32, (rows, reps), 0)
    group = row // ROWS_DEV
    spot, core = lax.rem(group, 8), group // 8
    chip = jnp.where(core == 0, chip_of(0, spot), chip_of(1, spot))
    holds = (2 * chip + core == lax.broadcasted_iota(jnp.int32, (rows, reps), 1)).astype(F32)
    counts = lax.dot_general(holds, c_ref[...].astype(F32), (((1,), (1,)), ((), ())), preferred_element_type=F32)
    spot = lax.rem(lax.broadcasted_iota(jnp.int32, (rows, 1), 0), ROWS_DEV).astype(F32)
    running = jnp.zeros_like(spot)
    version = jnp.zeros((rows, 1), jnp.int32)
    for v in range(POLICY_VERSIONS):
        running = running + counts[:, v : v + 1]
        version = version + (running <= spot).astype(jnp.int32)
    o_ref[...] = jnp.broadcast_to(version, o_ref.shape)


def partial(x_ref, d_ref, e_ref, v_ref, o_ref):
    chip, core = place()
    feats = d_ref.shape[1]
    mine = x_ref[:, pl.ds(pl.multiple_of((2 * chip + core) * feats, feats), feats)]
    other = x_ref[:, pl.ds(pl.multiple_of((2 * chip + 1 - core) * feats, feats), feats)]
    rows = x_ref.shape[0]
    version = v_ref[pl.ds(pl.multiple_of(core * rows, rows), rows), :]
    total = jnp.zeros(o_ref.shape, F32)
    for v in range(POLICY_VERSIONS):
        total = total + jnp.where(version == v, dot(mine, d_ref[v]) + dot(other, e_ref[v]), 0.0)
    o_ref[...] = total


def add(*refs):
    total = refs[0][...]
    for ref in refs[1:-1]:
        total = total + ref[...]
    refs[-1][...] = total


def finish(todo, x, have, totals, part, got, version, ag, au):
    rows, cols = totals[0].shape
    nt = len(todo)

    def body(x_ref, *refs):
        w_refs, (tg_ref, tu_ref, s_ref, r_ref, v_ref, ag_ref, au_ref, o_ref) = refs[:nt], refs[nt:]
        _, core = place()
        mine, other = s_ref[...], r_ref[...]
        shrink = jnp.concatenate([jnp.where(core == 0, mine, other), jnp.where(core == 0, other, mine)], axis=0)
        turned = pltpu.roll(shrink, ADAPTER_RANK, 1)
        column = lax.broadcasted_iota(jnp.int32, shrink.shape, 1)
        low = column < ADAPTER_RANK
        version = v_ref[...]
        half = (column >= ADAPTER_RANK).astype(jnp.int32)
        wide = []
        for twice in (jnp.where(low, shrink, turned), jnp.where(low, turned, shrink)):
            parts = [jnp.where(version == 2 * k + half, twice, 0.0).astype(BF16) for k in range(POLICY_VERSIONS // 2)]
            wide.append(jnp.concatenate(parts, axis=1))
        groups = rows // ROWS_DEV
        where = {}
        for core_ in range(2):
            for spot in range(groups // 2):
                where[2 * chip_of(core_, spot) + core_] = (core_ * (groups // 2) + spot) * ROWS_DEV
        for n in range(0, cols, 256):
            both = []
            for m, (t_ref, a_ref) in enumerate(((tg_ref, ag_ref), (tu_ref, au_ref))):
                total = t_ref[:, n : n + 256]
                for (m2, k), w_ref in zip(todo, w_refs):
                    if m2 == m:
                        total = total + dot(x_ref[:, k * UNIT : (k + 1) * UNIT], w_ref[:, n : n + 256])
                both.append(total + adapter_scale * dot(wide[m], a_ref[:, n : n + 256]))
            gate, up = both
            hidden = gate / (1.0 + jnp.exp(-gate)) * up
            for r in range(0, groups, 2):
                two = [hidden[where[k] : where[k] + ROWS_DEV] for k in (r, r + 1)]
                o_ref[r * ROWS_DEV : (r + 2) * ROWS_DEV, n : n + 256] = jnp.concatenate(two, axis=0).astype(BF16)

    ins = (x, *[have[t] for t in todo], *totals, part, got, version, ag, au)
    return call(body, like((rows, cols)), ins, vmem=ROOM[2])


def work(todo, x, have, units, hbm, totals, counts=None, maps=(), after=None):
    cols = hbm[0].shape[1]
    done = sorted({m for m, _ in todo})
    old = [m for m in done if totals[m] is not None]
    nt, nu = len(todo), len(units)

    def body(*refs):
        refs = list(refs)

        def take(n):
            got, refs[:] = refs[:n], refs[n:]
            return got

        take(1 if after is not None else 0)
        c_refs, map_refs = take(1 if counts is not None else 0), take(len(maps))
        x_refs, w_refs, hbm_refs = take(1 if nt else 0), take(nt), take(2)
        old_refs, new_refs = dict(zip(old, take(len(old)))), dict(zip(done, take(len(done))))
        to_refs, v_refs, got_refs = take(nu), take(len(c_refs)), take(len(maps))
        if c_refs:
            small = pltpu.make_async_copy(c_refs[0], refs[1], refs[2])
            small.start()
        copies = [
            pltpu.make_async_copy(
                hbm_refs[m].at[pl.ds(k * UNIT + h * UNIT // CUTS, UNIT // CUTS), :],
                to_ref.at[pl.ds(h * UNIT // CUTS, UNIT // CUTS), :],
                refs[0].at[CUTS * i + h],
            )
            for i, ((m, k), to_ref) in enumerate(zip(units, to_refs))
            for h in range(CUTS)
        ]
        copies += [pltpu.make_async_copy(f, t, refs[0].at[CUTS * nu + i]) for i, (f, t) in enumerate(zip(map_refs, got_refs))]
        for c in copies:
            c.start()
        if c_refs:
            small.wait()
            versions(refs[1], v_refs[0])

        @pl.when(lax.axis_index("rep") >= 0)
        def _():
            for m in done:
                for n in range(0, cols, 256):
                    total = old_refs[m][:, n : n + 256] if m in old_refs else None
                    for (m2, k), w_ref in zip(todo, w_refs):
                        if m2 == m:
                            term = dot(x_refs[0][:, k * UNIT : (k + 1) * UNIT], w_ref[:, n : n + 256])
                            total = term if total is None else total + term
                    new_refs[m][:, n : n + 256] = total

        for c in copies:
            c.wait()

    ins = ([x] if nt else []) + [have[t] for t in todo]
    specs = [VM] * len(ins) + [HB] * 2 + [VM] * len(old)
    ncopy = CUTS * nu + len(maps)
    scratch = [pltpu.SemaphoreType.DMA((ncopy,))] if ncopy else []
    ins, specs = [*maps, *ins], [HB] * len(maps) + specs
    if counts is not None:
        ins, specs = [counts, *ins], [HB, *specs]
        scratch += [pltpu.VMEM(counts.shape, counts.dtype), pltpu.SemaphoreType.DMA]
    if after is not None:
        ins, specs = [after, *ins], [VM, *specs]
    ins += hbm
    alias = {len(ins) + i: done.index(m) for i, m in enumerate(old)}
    ins += [totals[m] for m in old]
    rows = x.shape[0] if nt else 0
    outs = [like((rows, cols), F32) for _ in done] + [like((UNIT, cols)) for _ in units]
    if counts is not None:
        outs.append(like((counts.shape[1] * ROWS_DEV, 128), jnp.int32))
    outs += [like(f.shape) for f in maps]
    got = call(
        body, outs, ins, specs, scratch, vmem=ROOM[1], alias=alias,
        bytes_=COST,
    )
    for m, t in zip(done, got):
        totals[m] = t
    for unit, w in zip(units, got[len(done) :]):
        have[unit] = pltpu.with_memory_space_constraint(w, pltpu.VMEM)
    return got[len(done) + nu :]


def cores():
    return [(i, i ^ 1) for i in range(16)]


def lanes(step):
    return [(2 * c + k, 2 * (c ^ LANE_BITS[k][step]) + k) for c in range(8) for k in range(2)]


def chips(bits):
    return [(i, i ^ (2 * bits)) for i in range(16)]


def permute(x, pairs):
    return lax.ppermute(x, "rep", pairs)


def split(items, sizes):
    return [items[sum(sizes[:i]) : sum(sizes[: i + 1])] for i in range(len(sizes))]


def hold(*values):
    return lax.optimization_barrier(values)


def tuned(x, counts, g, u, down, ag, au):
    feats, cols = g.shape
    hbm = [pltpu.with_memory_space_constraint(w, pltpu.HBM) for w in (g, u)]
    rows = counts.shape[0] * ROWS_DEV
    order = [(m, k) for k in range(feats // UNIT) for m in range(2)]
    early = split(order, EARLY)
    late = split(order[sum(EARLY) + MID :], LATE)
    have, totals = {}, [None, None]
    a = x
    for step in range(3):
        r = permute(a, lanes(step))
        if step == 2:
            held = permute(a, cores())
        if step == 0:
            e = permute(down, cores())
            (version,) = work([], None, have, early[step], hbm, totals, pltpu.with_memory_space_constraint(counts.T, pltpu.HBM))
        else:
            work([], None, have, early[step], hbm, totals)
        last = early[step][-1]
        if step == 0:
            r, e, version, have[last] = hold(r, e, version, have[last])
        else:
            r, have[last] = hold(r, have[last])
        if step == 2:
            held, r = hold(held, r)
            other = permute(r, cores())
        a = call(functools.partial(double, step), like((a.shape[0] * 2, feats)), (a, r))
    part = call(partial, like((rows // 2, 128), F32), (a, down, e, version))
    got = permute(part, chips(SUM_BITS[0]))
    if MID:
        last = order[sum(EARLY) + MID - 1]
        work([], None, have, order[sum(EARLY) :][:MID], hbm, totals, after=part)
        other, have[last] = hold(other, have[last])
    x = call(join, like((rows, feats)), (a, held, other))
    turns = split(order, TURNS)
    wide = POLICY_VERSIONS * ADAPTER_RANK
    maps = [pltpu.with_memory_space_constraint(w.reshape(wide, cols), pltpu.HBM) for w in (ag, au)]
    for j in range(4):
        fetched = work(turns[j], x, have, late[j], hbm, totals, maps=maps if j == MAPS else ())
        if j == MAPS:
            maps = [pltpu.with_memory_space_constraint(w, pltpu.VMEM) for w in fetched]
        if j < 3:
            got, totals[0] = hold(got, totals[0])
            part = call(add, like((rows // 2, 128), F32), (part, got))
            got = permute(part, chips(SUM_BITS[j + 1]) if j < 2 else cores())
    return finish(turns[4], x, have, totals, part, got, version, *maps)


def row_versions(counts):
    running = jnp.cumsum(counts, axis=1)
    place = jnp.arange(ROWS_DEV, dtype=jnp.int32)
    version = jnp.sum((running[:, None, :] <= place[None, :, None]).astype(jnp.int32), axis=2)
    return version.reshape(-1)


def spread_rank(onehot, factors):
    total_rows = factors.shape[0]
    widened = onehot[:, :, None] * factors.astype(jnp.float32)[:, None, :]
    return widened.reshape(total_rows, POLICY_VERSIONS * ADAPTER_RANK).astype(jnp.bfloat16)


def general(
    normed_input_rows,
    counts,
    gate_weight_matrix,
    up_weight_matrix,
    adapter_down_weight,
    adapter_gate_weight,
    adapter_up_weight,
):
    version = row_versions(counts)
    onehot_all = (version[:, None] == jnp.arange(POLICY_VERSIONS, dtype=jnp.int32)[None, :]).astype(
        jnp.float32
    )
    hidden_local = gate_weight_matrix.shape[1]
    feat_count = adapter_down_weight.shape[1]
    feat_start = lax.axis_index("rep") * feat_count
    piece = lax.all_gather(normed_input_rows, "rep", axis=0, tiled=True)
    feat_slice = lax.dynamic_slice_in_dim(piece, feat_start, feat_count, 1)
    every_version_output = jnp.einsum(
        "tj,bjo->tbo", feat_slice, adapter_down_weight, preferred_element_type=jnp.float32
    )
    partial_sum = jnp.sum(every_version_output * onehot_all[:, :, None], axis=1)
    base_gate = jnp.dot(piece, gate_weight_matrix, preferred_element_type=jnp.float32)
    base_up = jnp.dot(piece, up_weight_matrix, preferred_element_type=jnp.float32)
    combined_down = jnp.concatenate([base_gate, base_up, partial_sum], axis=1)
    shrink = lax.psum(combined_down[:, 2 * hidden_local :], "rep").astype(jnp.bfloat16)
    expanded_gate = spread_rank(onehot_all, shrink[:, :ADAPTER_RANK])
    expanded_up = spread_rank(onehot_all, shrink[:, ADAPTER_RANK:])
    gate_output = combined_down[:, :hidden_local] + adapter_scale * jnp.dot(
        expanded_gate,
        adapter_gate_weight.reshape(POLICY_VERSIONS * ADAPTER_RANK, hidden_local),
        preferred_element_type=jnp.float32,
    )
    up_output = combined_down[:, hidden_local : 2 * hidden_local] + adapter_scale * jnp.dot(
        expanded_up,
        adapter_up_weight.reshape(POLICY_VERSIONS * ADAPTER_RANK, hidden_local),
        preferred_element_type=jnp.float32,
    )
    return (jax.nn.silu(gate_output) * up_output).astype(jnp.bfloat16)


def solution(mesh):
    placed = (
        P(("groups", "rep"), None),
        P("groups", None),
        P(None, "rep"),
        P(None, "rep"),
        P("groups", "rep", None),
        P("groups", None, "rep"),
        P("groups", None, "rep"),
    )
    local = tuned if mesh.shape["rep"] == 16 else general
    return jax.shard_map(local, mesh=mesh, in_specs=placed, out_specs=P("groups", "rep"), check_vma=False)
```
